32 devices in a mesh: groups: 2 (over y), branch: 4 (over z), head: 2 (over x), seq: 2 (over core).
Axes of the slice: x: 2, y: 2, z: 4, core: 2. Of those that a mesh axis runs over, the one named last changes fastest.
Arguments:
- queries: bfloat16 [32, 2, 64, 576], P(('groups', 'branch'), None, 'head'), parts along dimension 0, may hold values from -48 to 48
- kv_new: bfloat16 [32, 2, 576], P(('groups', 'branch')), parts along dimension 0, may hold values from -6 to 6
- cache: bfloat16 [1024, 128, 576], P(('groups', 'branch', 'seq')), parts along dimension 0, may hold values from -6 to 6
- block_list: int32 [32, 128], P('groups'), parts along dimension 0, may hold values from 0 to 511, as said below
- lengths: int32 [32], P('groups'), parts along dimension 0, may hold values from 128 to 16384
- parent: int32 [32], P('groups'), parts along dimension 0, may hold values from -1 to 14, as said below
- w_uv: bfloat16 [64, 512, 128], P('head'), may hold values from -6 to 6
- w_out: bfloat16 [8192, 3584], P('head', 'seq'), may hold values from -0.0625 to 0.0625
Outputs:
- branch_out: bfloat16 [32, 2, 3584], P(('groups', 'branch', 'head'), None, 'seq'), parts along dimension 0
The draws below stay inside these ranges and needn't reach their ends.
There are 2 independent parts, one for each index of `groups`. The reference program is written for one: setup_inputs(seed, part) draws one part's arguments, and reference() takes and returns one part's arrays. A program takes and returns all parts, laid end to end along the dimension named above; an argument that names none is the same for every part. Nothing has to cross between parts.
Inputs may be any that keep to these rules, and one draw needn't show every extreme that they name: `block_list`: each branch lists 128 distinct blocks; block g is held by device g // 64 in the order of branch+seq. The blocks listed by the 4 branches of one branch index include at most 16 distinct blocks of any one holder, and exactly 16 of some holder. parent[0] is -1 (no parent); every other branch b has a parent below b.
All inputs are finite; a program needn't handle non-finite values.
Results may differ from the reference program's by a relative error of at most 0.015.
Values may be sent and summed in bfloat16 or wider, within the bound.
A program may use at most 192 MiB of HBM per device.

```python
import jax
import jax.numpy as jnp
from jax import lax

HEADS = 64
LATENT = 512
ROPE = 64
VHEAD = 128
D_OUT = 3584
BT = 128
NB = 128
BR_DEV = 4
WIDTH = 576
BRANCHES = 16
CDEV = 8
SLOTS = 16
BLK_DEV = 64
BLOCKS = 512
N_BRANCH = 4


def pool_lists(key):
    key = jax.random.fold_in(key, 11)
    local_key, root_key, order_key = jax.random.split(key, 3)
    local_scores = jax.random.randint(local_key, (N_BRANCH, CDEV, BLK_DEV), 0, 1 << 20) * BLK_DEV + jnp.arange(BLK_DEV)
    local_pick = jnp.argsort(local_scores, axis=-1)[:, :, :SLOTS]
    pool = (jnp.arange(CDEV)[None, :, None] * BLK_DEV + local_pick).reshape(N_BRANCH, CDEV * SLOTS)
    roots = jax.random.randint(root_key, (N_BRANCH,), 0, CDEV)
    spots = jnp.arange(CDEV * SLOTS)
    order_scores = jax.random.randint(order_key, (N_BRANCH, BR_DEV, CDEV * SLOTS), 0, 1 << 20) * (CDEV * SLOTS) + spots
    forced = spots[None, :] // SLOTS == roots[:, None]
    order_scores = jnp.where(forced[:, None, :], spots - CDEV * SLOTS, order_scores)
    ordering = jnp.argsort(order_scores, axis=-1)[:, :, :NB]
    chosen = jnp.take_along_axis(jnp.broadcast_to(pool[:, None, :], order_scores.shape), ordering, axis=-1)
    return chosen.reshape(BRANCHES, NB).astype(jnp.int32)


def cache_rows(key):
    key = jax.random.fold_in(key, 21)
    base_key = jax.random.fold_in(key, 0)
    values = jnp.clip(jax.random.normal(base_key, (BLOCKS, BT, WIDTH), jnp.float32), -6.0, 6.0)
    mixed_row = jnp.clip(values[:, 1, :], -6.0, 6.0)
    return values.at[:, 1, :].set(mixed_row)


def draw_block_list(key, part):
    return pool_lists(key)


def draw_cache(key, part):
    return cache_rows(key).astype(jnp.bfloat16)


def draw_queries(key, part):
    own_key = jax.random.fold_in(key, 31)
    values = jnp.clip(jax.random.normal(own_key, (BRANCHES, 2, HEADS, WIDTH), jnp.float32), -6.0, 6.0)
    return values.astype(jnp.bfloat16)


def draw_parent(key, part):
    key = jax.random.fold_in(key, 41)
    raw = jax.random.randint(key, (BRANCHES,), 0, 1 << 20)
    spots = jnp.arange(BRANCHES)
    return jnp.where(spots == 0, -1, raw % jnp.maximum(spots, 1)).astype(jnp.int32)


def touch_ends(entries, key, smallest, top_value):
    place = [jax.random.randint(jax.random.fold_in(key, axis), (), 0, length) for axis, length in enumerate(entries.shape)]
    widest = entries.shape.index(max(entries.shape))
    next_to = place[:widest] + [(place[widest] + 1) % entries.shape[widest]] + place[widest + 1:]
    return entries.at[tuple(place)].set(smallest).at[tuple(next_to)].set(top_value)


def steps_of(key, extent, cuts, low, largest):
    level = 1.0
    for dim, shards_of in cuts:
        draws = jax.random.uniform(jax.random.fold_in(jax.random.fold_in(key, 6), dim), (shards_of,), jnp.float32, low / len(cuts), largest / len(cuts))
        level = level * jnp.repeat(jnp.exp(draws), extent[dim] // shards_of).reshape((-1,) + (1,) * (len(extent) - 1 - dim))
    return level


def gaussian(stream_key, extent, spread, bound, shards=(), kind=jnp.bfloat16):
    drawn = jax.random.normal(stream_key, extent, jnp.float32) * spread
    if len(shards) > 0:
        drawn = steps_of(stream_key, extent, shards, -0.22, 0.18) * drawn
    return jnp.clip(drawn, min=-bound, max=bound).astype(kind)


def setup_inputs(seed: int = 0, part: int = 0) -> dict:
    splits = jax.random.split(jax.random.key(seed), 9)
    own_keys = jax.random.split(jax.random.fold_in(splits[8], part), 9)
    return {
        "queries": draw_queries(jax.random.fold_in(jax.random.fold_in(splits[8], part), 71), part),
        "kv_new": gaussian(own_keys[1], (BRANCHES, 2, WIDTH), 1.0, 6.0, ((0, 4),)),
        "cache": draw_cache(jax.random.fold_in(jax.random.fold_in(splits[8], part), 71), part),
        "block_list": draw_block_list(jax.random.fold_in(jax.random.fold_in(splits[8], part), 71), part),
        "lengths": touch_ends(jax.random.randint(own_keys[4], (BRANCHES,), BT, NB * BT + 1), jax.random.fold_in(own_keys[4], 1), BT, NB * BT).astype(jnp.int32),
        "parent": draw_parent(jax.random.fold_in(jax.random.fold_in(splits[8], part), 71), part),
        "w_uv": gaussian(splits[6], (HEADS, LATENT, VHEAD), 1.0, 6.0, ((0, 2),)),
        "w_out": gaussian(splits[7], (HEADS * VHEAD, D_OUT), (HEADS * VHEAD) ** -0.5, 0.0625, ((0, 2), (1, 2))),
    }


def reference(queries, kv_new, cache, block_list, lengths, parent, w_uv, w_out):
    qk_scale = float(VHEAD + ROPE) ** -0.5
    context_len = NB * BT
    wide_uv = w_uv.astype(jnp.float32)
    draft_pos = jnp.arange(2)
    own_mask = draft_pos[None, :] <= draft_pos[:, None]

    def one_branch(branch_id):
        block_ids = block_list[branch_id]
        context = cache[block_ids].reshape(context_len, WIDTH)
        parent_id = parent[branch_id]
        parent_rows = kv_new[jnp.maximum(parent_id, 0)]
        own_rows = kv_new[branch_id]
        key_rows = jnp.concatenate([context, parent_rows, own_rows], axis=0)
        context_vis = jnp.broadcast_to((jnp.arange(context_len) < lengths[branch_id])[None, :], (2, context_len))
        parent_vis = jnp.broadcast_to(parent_id >= 0, (2, 2))
        visible = jnp.concatenate([context_vis, parent_vis, own_mask], axis=1)
        scores = jnp.einsum("tha,ka->thk", queries[branch_id].astype(jnp.float32), key_rows.astype(jnp.float32)) * qk_scale
        scores = jnp.where(visible[:, None, :], scores, -1e30)
        peak = jnp.max(scores, axis=-1, keepdims=True)
        exps = jnp.where(visible[:, None, :], jnp.exp(scores - peak), 0.0)
        totals = jnp.sum(exps, axis=-1)
        weights = exps.astype(jnp.bfloat16)
        summed = jnp.einsum("thk,kc->thc", weights.astype(jnp.float32), key_rows[:, :LATENT].astype(jnp.float32))
        latent_out = summed / totals[:, :, None]
        head_out = jnp.einsum("thc,hcv->thv", latent_out, wide_uv, precision=lax.Precision.HIGHEST).astype(jnp.bfloat16)
        flattened = head_out.reshape(2, HEADS * VHEAD)
        return jnp.dot(flattened, w_out, preferred_element_type=jnp.float32).astype(jnp.bfloat16)

    return lax.map(one_branch, jnp.arange(BRANCHES, dtype=jnp.int32))
```

```python
import jax
import jax.numpy as jnp
from jax import lax
from jax.sharding import PartitionSpec as P

ROPE = 64
VHEAD = 128


def slots_of(block_list, lengths, my_index, block_count, block_len, rows, slots):
    mine = block_list - my_index * block_count
    lead = mine[::rows]
    held = (lead >= 0) & (lead < block_count)
    spots = jnp.arange(mine.shape[1])
    before = spots[None, :] < spots[:, None]
    rank = jnp.sum((held[:, None, :] & before[None]).astype(jnp.int32), axis=2)
    slot = jnp.arange(slots)
    chosen = held[:, None, :] & (rank[:, None, :] == slot[None, :, None])
    ids = jnp.sum(jnp.where(chosen, lead[:, None, :], 0), axis=2)
    all_ids = jnp.repeat(ids, rows, axis=0)
    match = mine[:, None, :] == all_ids[:, :, None]
    place = jnp.sum(jnp.where(match, spots, 0), axis=2)
    room = lengths[:, None] - place * block_len
    bias = jnp.where(jnp.arange(block_len) < room[:, :, None], 0.0, -1e30)
    return ids, bias.reshape(mine.shape[0], slots * block_len)


def local(queries, kv_new, cache, block_list, lengths, parent, w_uv, w_out):
    rows, _, heads, feature = queries.shape
    block_count, block_len, _ = cache.shape
    latent = w_uv.shape[1]
    branch_count = lax.axis_size("branch")
    seq_count = lax.axis_size("seq")
    head_count = lax.axis_size("head")
    branch_at = lax.axis_index("branch")
    my_index = branch_at * seq_count + lax.axis_index("seq")
    slots = block_list.shape[1] // (branch_count * seq_count)
    scale = float(VHEAD + ROPE) ** (-0.5) * 1.4426950408889634
    ids, bias = slots_of(block_list, lengths, my_index, block_count, block_len, rows, slots)
    everyone = lax.all_gather(queries, "branch", axis=0)
    keys = jnp.take(cache, ids.reshape(-1), axis=0).reshape(branch_count, slots * block_len, feature)
    scores = jnp.einsum(
        "brtha,bka->brthk", everyone, keys, preferred_element_type=jnp.float32
    ) * scale
    scores = scores + bias.reshape(branch_count, rows, 1, 1, -1)
    peak = jnp.max(scores, axis=-1)
    exps = jnp.exp2(scores - peak[..., None])
    totals = jnp.sum(exps, axis=-1)
    summed = jnp.einsum(
        "brthk,bkc->brthc",
        exps.astype(jnp.bfloat16),
        keys[:, :, :latent],
        preferred_element_type=jnp.float32,
    ).astype(jnp.bfloat16)
    stats = jnp.stack([peak, totals], axis=1)
    summed = lax.all_to_all(summed, "branch", 0, 0, tiled=True)
    stats = lax.all_to_all(stats, "branch", 0, 0, tiled=True)
    summed = lax.all_gather(summed, "seq", axis=0, tiled=True)
    stats = lax.all_gather(stats, "seq", axis=0, tiled=True)
    new_keys = lax.all_gather(kv_new, "branch", axis=0, tiled=True)
    parents = lax.dynamic_slice_in_dim(parent, branch_at * rows, rows)
    own = branch_at * rows + jnp.arange(rows)
    which = jnp.arange(new_keys.shape[0])
    draft = jnp.arange(2)
    seen = (which[None, :] == parents[:, None])[:, None, :, None] | (
        (which[None, :] == own[:, None])[:, None, :, None]
        & (draft[None, :] <= draft[:, None])[None, :, None, :]
    )
    new_scores = jnp.einsum(
        "rtha,bua->rthbu", queries, new_keys, preferred_element_type=jnp.float32
    ) * scale
    new_scores = jnp.where(seen[:, :, None], new_scores, -1e30)
    new_scores = new_scores.reshape(rows, 2, heads, -1)
    top = jnp.maximum(jnp.max(stats[:, 0], axis=0), jnp.max(new_scores, axis=-1))
    new_exps = jnp.exp2(new_scores - top[..., None])
    part = jnp.exp2(stats[:, 0] - top[None])
    total = jnp.sum(part * stats[:, 1], axis=0) + jnp.sum(new_exps, axis=-1)
    latent_out = jnp.sum(part[..., None] * summed.astype(jnp.float32), axis=0) + jnp.einsum(
        "rthk,kc->rthc",
        new_exps.astype(jnp.bfloat16),
        new_keys.reshape(-1, feature)[:, :latent],
        preferred_element_type=jnp.float32,
    )
    latent_out = latent_out / total[..., None]
    head_out = jnp.einsum(
        "rthc,hcv->rthv",
        latent_out,
        w_uv.astype(jnp.float32),
        precision=lax.Precision.HIGHEST,
    ).astype(jnp.bfloat16)
    result = jnp.dot(
        head_out.reshape(rows * 2, -1), w_out, preferred_element_type=jnp.float32
    )
    return lax.psum_scatter(
        result.reshape(rows, 2, w_out.shape[1]).astype(jnp.bfloat16),
        "head",
        scatter_dimension=0,
        tiled=True,
    )


def solution(mesh):
    return jax.shard_map(
        local,
        mesh=mesh,
        in_specs=(
            P(("groups", "branch"), None, "head", None),
            P(("groups", "branch"), None, None),
            P(("groups", "branch", "seq"), None, None),
            P("groups", None),
            P("groups"),
            P("groups"),
            P("head", None, None),
            P("head", "seq"),
        ),
        out_specs=P(("groups", "branch", "head"), None, "seq"),
        check_vma=False,
    )
```

```python
import functools

import jax
import jax.numpy as jnp
from jax import lax
from jax.experimental import pallas as pl
from jax.experimental.pallas import tpu as pltpu
from jax.sharding import PartitionSpec as P

ROPE = 64
VHEAD = 128
MESH = pl.DeviceIdType.MESH
LOW = -1e30


def slots_of(block_list, lengths, my_index, block_count, block_len, rows, slots):
    mine = block_list - my_index * block_count
    lead = mine[::rows]
    held = (lead >= 0) & (lead < block_count)
    spots = jnp.arange(mine.shape[1])
    before = spots[None, :] < spots[:, None]
    rank = jnp.sum((held[:, None, :] & before[None]).astype(jnp.int32), axis=2)
    slot = jnp.arange(slots)
    chosen = held[:, None, :] & (rank[:, None, :] == slot[None, :, None])
    ids = jnp.sum(jnp.where(chosen, lead[:, None, :], 0), axis=2)
    all_ids = jnp.repeat(ids, rows, axis=0)
    match = mine[:, None, :] == all_ids[:, :, None]
    place = jnp.sum(jnp.where(match, spots, 0), axis=2)
    room = lengths[:, None] - place * block_len
    bias = jnp.where(jnp.arange(block_len) < room[:, :, None], 0.0, LOW)
    return ids, bias.reshape(-1, rows, slots * block_len)


def as_row(column):
    short = 128 - column.shape[0]
    if short > 0:
        column = jnp.concatenate([column, jnp.zeros((short, 128), jnp.float32)], axis=0)
    return jnp.transpose(column)[:8]


def as_columns(rows_in, height):
    lane = lax.broadcasted_iota(jnp.int32, (128, rows_in[0].shape[1]), 0)
    stacked = jnp.zeros(lane.shape, jnp.float32)
    for j, row in enumerate(rows_in):
        stacked = jnp.where(lane == j, row[0:1], stacked)
    return jnp.transpose(stacked)[:height]


def pair_row(peak, total):
    lane = lax.broadcasted_iota(jnp.int32, (peak.shape[0], 128), 1)
    return as_row(jnp.where(lane == 0, peak, total))


def kernel(
    scale,
    rows,
    ids_ref,
    bias_ref,
    new_bias_ref,
    q_ref,
    kv_ref,
    cache_ref,
    uv_ref,
    out_w_ref,
    out_ref,
    cache_v,
    uv_v,
    out_v,
    q_all,
    kv_all,
    keys,
    scores,
    probs,
    column,
    o_out,
    o_in,
    s_out,
    s_in,
    z_out,
    z_in,
    zs_out,
    zs_in,
    latent_v,
    head_v,
    red_out,
    red_in,
    local_sem,
    q_send,
    q_recv,
    f_send,
    f_recv,
    kv_send,
    kv_recv,
    o_send,
    o_recv,
    s_send,
    s_recv,
    z_send,
    z_recv,
    zs_send,
    zs_recv,
    h_send,
    h_recv,
    r_send,
    r_recv,
):
    nb, hc = lax.axis_size("branch"), lax.axis_size("head")
    z, x, core = lax.axis_index("branch"), lax.axis_index("head"), lax.axis_index("seq")
    other = 1 - core
    height, feature = q_ref.shape[1], q_ref.shape[2]
    block_len = cache_v.shape[1]
    slots = ids_ref.shape[1]
    latent = uv_v.shape[1]
    heads = uv_v.shape[0]
    groups = rows * 2

    cache_copy = pltpu.make_async_copy(cache_ref, cache_v, local_sem.at[0])
    cache_copy.start()
    uv_copy = pltpu.make_async_copy(uv_ref.at[pl.ds(core * heads, heads)], uv_v, local_sem.at[1])
    uv_copy.start()
    depth = out_v.shape[1]
    out_copies = []
    for g in range(2):
        out_copies.append(
            pltpu.make_async_copy(
                out_w_ref.at[pl.ds(g * depth, depth)], out_v.at[g], local_sem.at[2 + g]
            )
        )
        out_copies[-1].start()

    barrier = pltpu.get_barrier_semaphore()
    for d in range(1, nb):
        pl.semaphore_signal(
            barrier, inc=1, device_id={"branch": lax.rem(z + d, nb)}, device_id_type=MESH
        )
    for e in range(1, hc):
        pl.semaphore_signal(
            barrier, inc=1, device_id={"head": lax.rem(x + e, hc)}, device_id_type=MESH
        )
    pl.semaphore_signal(barrier, inc=1, device_id={"seq": other}, device_id_type=MESH)
    pl.semaphore_wait(barrier, nb - 1 + hc - 1 + 1)

    def remote(src, dst, send, recv, target):
        return pltpu.make_async_remote_copy(
            src_ref=src,
            dst_ref=dst,
            send_sem=send,
            recv_sem=recv,
            device_id=target,
            device_id_type=MESH,
        )

    sent = []

    def go(copy):
        copy.start()
        sent.append(copy)
        return copy

    q_copies, kv_copies = [None], [None]
    for d in range(1, nb):
        there = {"branch": lax.rem(z + d, nb)}
        q_copies.append(
            go(remote(q_ref.at[core], q_all.at[d, core], q_send.at[d], q_recv.at[d], there))
        )
    for d in range(1, nb):
        there = {"branch": lax.rem(z + d, nb)}
        kv_copies.append(go(remote(kv_ref, kv_all.at[d], kv_send.at[d], kv_recv.at[d], there)))
    kv_all[0] = kv_ref[...]

    o_copies, s_copies, z_copies, zs_copies = [], [], [None], [None]

    def attend(d):
        source = lax.rem(z + nb - d, nb)
        for s in range(slots):
            keys[s * block_len : (s + 1) * block_len, :] = cache_v[ids_ref[source, s]]
        q = (q_ref if d == 0 else q_all.at[d])[...].reshape(2 * height, feature)
        scores[...] = lax.dot_general(
            q, keys[...], (((1,), (1,)), ((), ())), preferred_element_type=jnp.float32
        )
        size = height // rows
        for g in range(2):
            for r in range(rows):
                at = g * height + r * size
                v = scores[at : at + size, :] * scale + bias_ref[source, r : r + 1, :]
                peak = jnp.max(v, axis=1, keepdims=True)
                p = jnp.exp2(v - peak)
                total = jnp.sum(p, axis=1, keepdims=True)
                probs[at : at + size, :] = p.astype(jnp.bfloat16)
                lane = lax.broadcasted_iota(jnp.int32, (size, 128), 1)
                column[at : at + size, :] = jnp.where(lane == 0, peak, total)
        for g in range(2):
            s_out[d, g] = as_row(column[g * height : (g + 1) * height, :])
        summed = jnp.dot(probs[...], keys[:, :latent], preferred_element_type=jnp.float32)
        o_out[d] = summed.astype(jnp.bfloat16).reshape(2, height, latent)
        partner = {"seq": other}
        s_copies.append(go(remote(s_out.at[d, other], s_in.at[d], s_send.at[d], s_recv.at[d], partner)))
        o_copies.append(go(remote(o_out.at[d, other], o_in.at[d], o_send.at[d], o_recv.at[d], partner)))

    def merge(d):
        s_copies[d].wait_recv()
        one, two = s_out[d, core], s_in[d]
        top = jnp.maximum(one[0:1], two[0:1])
        c1, c2 = jnp.exp2(one[0:1] - top), jnp.exp2(two[0:1] - top)
        total = one[1:2] * c1 + two[1:2] * c2
        line = lax.broadcasted_iota(jnp.int32, zs_out.shape[1:], 0)
        zs_out[d] = jnp.where(line == 0, top, total)
        cols = as_columns([c1, c2], height)
        o_copies[d].wait_recv()
        merged = o_out[d, core].astype(jnp.float32) * cols[:, 0:1] + o_in[d].astype(
            jnp.float32
        ) * cols[:, 1:2]
        z_out[d] = merged.astype(jnp.bfloat16)
        if d > 0:
            there = {"branch": lax.rem(z + nb - d, nb)}
            zs_copies.append(
                go(remote(zs_out.at[d], zs_in.at[d], zs_send.at[d], zs_recv.at[d], there))
            )
            z_copies.append(go(remote(z_out.at[d], z_in.at[d], z_send.at[d], z_recv.at[d], there)))

    cache_copy.wait()
    forwards = [None]
    attend(0)
    for d in range(1, nb):
        q_copies[d].wait_recv()
        forward = go(
            remote(
                q_all.at[d, core], q_all.at[d, core], f_send.at[d], f_recv.at[d], {"seq": other}
            )
        )
        merge(d - 1)
        forward.wait_recv()
        attend(d)
    merge(nb - 1)

    for d in range(1, nb):
        kv_copies[d].wait_recv()
    new_keys = kv_all[...].reshape(-1, feature)
    size = height // groups
    new_scores = lax.dot_general(
        q_ref[core], new_keys, (((1,), (1,)), ((), ())), preferred_element_type=jnp.float32
    )
    new_v = new_scores.reshape(groups, size, -1) * scale + new_bias_ref[...][:, None, :]
    new_v = new_v.reshape(height, -1)
    new_peak = jnp.max(new_v, axis=1, keepdims=True)
    new_p = jnp.exp2(new_v - new_peak)
    new_total = jnp.sum(new_p, axis=1, keepdims=True)
    new_row = pair_row(new_peak, new_total)
    new_sum = jnp.dot(
        new_p.astype(jnp.bfloat16), new_keys[:, :latent], preferred_element_type=jnp.float32
    )

    stats = [zs_out[0], new_row]
    for d in range(1, nb):
        zs_copies[d].wait_recv()
        stats.append(zs_in[d])
    top = functools.reduce(jnp.maximum, [s[0:1] for s in stats])
    shares = [jnp.exp2(s[0:1] - top) for s in stats]
    total = sum(c * s[1:2] for c, s in zip(shares, stats))
    cols = as_columns([c / total for c in shares], height)
    latent_out = z_out[0].astype(jnp.float32) * cols[:, 0:1] + new_sum * cols[:, 1:2]
    for d in range(1, nb):
        z_copies[d].wait_recv()
        latent_out = latent_out + z_in[d].astype(jnp.float32) * cols[:, d + 1 : d + 2]
    for j in range(latent // 128):
        latent_v[j] = latent_out[:, j * 128 : (j + 1) * 128]

    uv_copy.wait()
    for h in range(heads):
        part = jnp.concatenate(
            [latent_v[j, pl.ds(h, groups, stride=heads), :] for j in range(latent // 128)], axis=1
        )
        high = part.astype(jnp.bfloat16)
        rest = (part - high.astype(jnp.float32)).astype(jnp.bfloat16)
        both = jnp.dot(
            jnp.concatenate([high, rest], axis=0), uv_v[h], preferred_element_type=jnp.float32
        )
        up = both[:groups] + both[groups:]
        head_v[core, :, h * VHEAD : (h + 1) * VHEAD] = jnp.concatenate([up, up], axis=0).astype(
            jnp.bfloat16
        )
    swap = go(
        remote(head_v.at[core], head_v.at[core], h_send.at[0], h_recv.at[0], {"seq": other})
    )
    for copy in out_copies:
        copy.wait()
    result = jnp.dot(head_v[core], out_v[core], preferred_element_type=jnp.float32)
    swap.wait_recv()
    result = result + jnp.dot(head_v[other], out_v[other], preferred_element_type=jnp.float32)
    result = result[:groups]
    red_out[...] = result
    reds = []
    for e in range(1, hc):
        there = {"head": lax.rem(x + e, hc)}
        reds.append(
            go(remote(red_out, red_in.at[e - 1], r_send.at[e - 1], r_recv.at[e - 1], there))
        )
    for e in range(1, hc):
        reds[e - 1].wait_recv()
        result = result + red_in[e - 1]
    count = out_ref.shape[0]
    mine = jnp.zeros(out_ref.shape, jnp.float32)
    for k in range(hc):
        mine = jnp.where(x == k, result[k * count : (k + 1) * count], mine)
    out_ref[...] = mine.astype(out_ref.dtype)
    for copy in sent:
        copy.wait_send()


def local(queries, kv_new, cache, block_list, lengths, parent, w_uv, w_out):
    rows, _, heads, feature = queries.shape
    block_count, block_len, _ = cache.shape
    latent = w_uv.shape[1]
    nb = lax.axis_size("branch")
    ns = lax.axis_size("seq")
    hc = lax.axis_size("head")
    branch_at = lax.axis_index("branch")
    my_index = branch_at * ns + lax.axis_index("seq")
    slots = block_list.shape[1] // (nb * ns)
    scale = float(VHEAD + ROPE) ** (-0.5) * 1.4426950408889634
    ids, bias = slots_of(block_list, lengths, my_index, block_count, block_len, rows, slots)
    half = heads // 2
    groups = rows * 2
    height = groups * half
    q = queries.reshape(groups, 2, half, feature).transpose(1, 0, 2, 3)
    q = q.reshape(2, height, feature)
    pad = 16
    kv = jnp.pad(kv_new.reshape(groups, feature), ((0, pad - groups), (0, 0)))

    parents = lax.dynamic_slice_in_dim(parent, branch_at * rows, rows)
    spot = jnp.arange(nb * pad)
    origin = (branch_at - spot // pad + nb) % nb
    inner = spot % pad
    which = jnp.where(inner < groups, origin * rows + inner // 2, -2)
    own = branch_at * rows + jnp.arange(rows)
    seen = (which[None, None, :] == parents[:, None, None]) | (
        (which[None, None, :] == own[:, None, None])
        & ((inner % 2)[None, None, :] <= jnp.arange(2)[None, :, None])
    )
    new_bias = jnp.where(seen, 0.0, LOW).reshape(groups, nb * pad)

    depth = w_out.shape[0] // 2
    width = w_out.shape[1]
    dma = pltpu.SemaphoreType.DMA
    vmem = pl.BlockSpec(memory_space=pltpu.VMEM)
    hbm = pl.BlockSpec(memory_space=pl.ANY)
    count = groups // hc
    bf16, f32 = jnp.bfloat16, jnp.float32
    out = pl.pallas_call(
        functools.partial(kernel, scale, rows),
        out_shape=jax.ShapeDtypeStruct((count, width), bf16),
        in_specs=[
            pl.BlockSpec(memory_space=pltpu.SMEM),
            vmem,
            vmem,
            vmem,
            vmem,
            hbm,
            hbm,
            hbm,
        ],
        out_specs=vmem,
        scratch_shapes=[
            pltpu.VMEM((block_count, block_len, feature), bf16),
            pltpu.VMEM((half, latent, VHEAD), bf16),
            pltpu.VMEM((2, depth, width), bf16),
            pltpu.VMEM((nb, 2, height, feature), bf16),
            pltpu.VMEM((nb, pad, feature), bf16),
            pltpu.VMEM((slots * block_len, feature), bf16),
            pltpu.VMEM((2 * height, slots * block_len), f32),
            pltpu.VMEM((2 * height, slots * block_len), bf16),
            pltpu.VMEM((2 * height, 128), f32),
            pltpu.VMEM((nb, 2, height, latent), bf16),
            pltpu.VMEM((nb, height, latent), bf16),
            pltpu.VMEM((nb, 2, 8, 128), f32),
            pltpu.VMEM((nb, 8, 128), f32),
            pltpu.VMEM((nb, height, latent), bf16),
            pltpu.VMEM((nb, height, latent), bf16),
            pltpu.VMEM((nb, 8, 128), f32),
            pltpu.VMEM((nb, 8, 128), f32),
            pltpu.VMEM((latent // 128, height, 128), f32),
            pltpu.VMEM((2, 2 * groups, half * VHEAD), bf16),
            pltpu.VMEM((groups, width), f32),
            pltpu.VMEM((hc, groups, width), f32),
            dma((4,)),
        ]
        + [dma((nb,)) for _ in range(14)]
        + [dma((1,)), dma((1,)), dma((hc,)), dma((hc,))],
        compiler_params=pltpu.CompilerParams(
            collective_id=0, has_side_effects=True, vmem_limit_bytes=56 * 1024 * 1024
        ),
    )(ids, bias, new_bias, q, kv, cache, w_uv, w_out)
    return out.reshape(rows // hc, 2, width)


def solution(mesh):
    return jax.shard_map(
        local,
        mesh=mesh,
        in_specs=(
            P(("groups", "branch"), None, "head", None),
            P(("groups", "branch"), None, None),
            P(("groups", "branch", "seq"), None, None),
            P("groups", None),
            P("groups"),
            P("groups"),
            P("head", None, None),
            P("head", "seq"),
        ),
        out_specs=P(("groups", "branch", "head"), None, "seq"),
        check_vma=False,
    )
```

```python
import functools

import jax
import jax.numpy as jnp
from jax import lax
from jax.experimental import pallas as pl
from jax.experimental.pallas import tpu as pltpu
from jax.sharding import PartitionSpec as P

ROPE = 64
VHEAD = 128
MESH = pl.DeviceIdType.MESH
LOW = -1e30


def as_row(column):
    short = 128 - column.shape[0]
    if short > 0:
        column = jnp.concatenate([column, jnp.zeros((short, 128), jnp.float32)], axis=0)
    return jnp.transpose(column)[:8]


def as_columns(rows_in, height):
    lane = lax.broadcasted_iota(jnp.int32, (128, rows_in[0].shape[1]), 0)
    stacked = jnp.zeros(lane.shape, jnp.float32)
    for j, row in enumerate(rows_in):
        stacked = jnp.where(lane == j, row[0:1], stacked)
    return jnp.transpose(stacked)[:height]


def pair_row(peak, total):
    lane = lax.broadcasted_iota(jnp.int32, (peak.shape[0], 128), 1)
    return as_row(jnp.where(lane == 0, peak, total))


def kernel(
    scale,
    rows,
    list_ref,
    lengths_ref,
    parent_ref,
    q_ref,
    kv_ref,
    cache_ref,
    uv_ref,
    out_w_ref,
    out_ref,
    cache_v,
    uv_v,
    out_v,
    q_all,
    kv_all,
    keys,
    scores,
    probs,
    column,
    o_out,
    o_in,
    s_out,
    s_in,
    z_out,
    z_in,
    zs_out,
    zs_in,
    latent_v,
    ids_v,
    ids_s,
    bias_v,
    kv_v,
    head_v,
    red_out,
    red_in,
    local_sem,
    q_send,
    q_recv,
    f_send,
    f_recv,
    kv_send,
    kv_recv,
    o_send,
    o_recv,
    s_send,
    s_recv,
    z_send,
    z_recv,
    zs_send,
    zs_recv,
    h_send,
    h_recv,
    r_send,
    r_recv,
):
    nb, hc = lax.axis_size("branch"), lax.axis_size("head")
    z, x, core = lax.axis_index("branch"), lax.axis_index("head"), lax.axis_index("seq")
    other = 1 - core
    block_count, feature, block_len = cache_v.shape
    branches, list_len = list_ref.shape
    slots = list_len // (nb * 2)
    latent = uv_v.shape[1]
    heads = uv_v.shape[0]
    groups = rows * 2
    height = groups * heads

    def q_half(g):
        if len(q_ref.shape) == 4:
            return q_ref.at[g]
        return q_ref.at[:, pl.ds(pl.multiple_of(g * heads, heads), heads), :]

    cache_copy = pltpu.make_async_copy(cache_ref, cache_v, local_sem.at[0])
    cache_copy.start()
    uv_copy = pltpu.make_async_copy(uv_ref.at[pl.ds(core * heads, heads)], uv_v, local_sem.at[1])
    uv_copy.start()
    barrier = pltpu.get_barrier_semaphore()
    for d in range(1, nb):
        pl.semaphore_signal(
            barrier, inc=1, device_id={"branch": lax.rem(z + d, nb)}, device_id_type=MESH
        )
    for e in range(1, hc):
        pl.semaphore_signal(
            barrier, inc=1, device_id={"head": lax.rem(x + e, hc)}, device_id_type=MESH
        )
    pl.semaphore_signal(barrier, inc=1, device_id={"seq": other}, device_id_type=MESH)

    drafts = [kv_ref[r].astype(jnp.float32) for r in range(rows)]
    drafts.append(jnp.zeros((kv_v.shape[0] - groups, feature), jnp.float32))
    kv_v[...] = jnp.concatenate(drafts, axis=0).astype(jnp.bfloat16)
    pl.semaphore_wait(barrier, nb - 1 + hc - 1 + 1)

    def remote(src, dst, send, recv, target):
        return pltpu.make_async_remote_copy(
            src_ref=src,
            dst_ref=dst,
            send_sem=send,
            recv_sem=recv,
            device_id=target,
            device_id_type=MESH,
        )

    sent = []

    def go(copy):
        copy.start()
        sent.append(copy)
        return copy

    q_copies, kv_copies = [None], [None]
    for d in range(1, nb):
        there = {"branch": lax.rem(z + d, nb)}
        q_copies.append(
            go(remote(q_half(core), q_all.at[d, core], q_send.at[d], q_recv.at[d], there))
        )
    for d in range(1, nb):
        there = {"branch": lax.rem(z + d, nb)}
        kv_copies.append(go(remote(kv_v, kv_all.at[d], kv_send.at[d], kv_recv.at[d], there)))
    kv_all[0] = kv_v[...]

    mine = list_ref[...] - (z * 2 + core) * block_count
    lead = jnp.concatenate(
        [
            jnp.broadcast_to(mine[i * rows : i * rows + 1], (rows, list_len))
            for i in range(nb)
        ],
        axis=0,
    )
    held = (lead >= 0) & (lead < block_count)
    spots = lax.broadcasted_iota(jnp.int32, (branches, list_len), 1)
    line = lax.broadcasted_iota(jnp.int32, (branches, list_len), 0)
    counted = held.astype(jnp.int32)
    rank = counted
    step = 1
    while step < list_len:
        rank = rank + jnp.where(spots >= step, pltpu.roll(rank, step, 1), 0)
        step *= 2
    rank = jnp.where(held, rank - 1, -1)
    reach = jnp.zeros((branches, list_len), jnp.int32)
    for b in range(branches):
        reach = jnp.where(line == b, lengths_ref[b], reach)
    table = jnp.zeros((branches, list_len), jnp.int32)
    picks = []
    for s in range(slots):
        pick = jnp.sum(jnp.where(rank == s, lead, 0), axis=1, keepdims=True)
        picks.append(pick)
        table = jnp.where(spots == s, pick, table)
    ids_v[...] = table
    ids_copy = pltpu.make_async_copy(ids_v, ids_s, local_sem.at[4])
    ids_copy.start()
    for s in range(slots):
        place = jnp.sum(jnp.where(mine == picks[s], spots, 0), axis=1, keepdims=True)
        seen = spots + place * block_len < reach
        bias_v[:, s * block_len : (s + 1) * block_len] = jnp.where(seen, 0.0, LOW)
    ids_copy.wait()

    o_copies, s_copies, z_copies, zs_copies = [], [], [None], [None]

    def attend(d):
        source = lax.rem(z + nb - d, nb)
        for s in range(slots):
            keys[:, s * block_len : (s + 1) * block_len] = cache_v[ids_s[source * rows, s]]
        if d == 0:
            q = jnp.concatenate(
                [q_half(g)[...].reshape(height, feature) for g in range(2)], axis=0
            )
        else:
            q = q_all[d].reshape(2 * height, feature)
        scores[...] = jnp.dot(q, keys[...], preferred_element_type=jnp.float32)
        size = height // rows
        for g in range(2):
            for r in range(rows):
                at = g * height + r * size
                v = scores[at : at + size, :] * scale + bias_v[pl.ds(source * rows + r, 1), :]
                peak = jnp.max(v, axis=1, keepdims=True)
                p = jnp.exp2(v - peak)
                total = jnp.sum(p, axis=1, keepdims=True)
                probs[at : at + size, :] = p.astype(jnp.bfloat16)
                lane = lax.broadcasted_iota(jnp.int32, (size, 128), 1)
                column[at : at + size, :] = jnp.where(lane == 0, peak, total)
        for g in range(2):
            s_out[d, g] = as_row(column[g * height : (g + 1) * height, :])
        summed = lax.dot_general(
            probs[...],
            keys[:latent, :],
            (((1,), (1,)), ((), ())),
            preferred_element_type=jnp.float32,
        )
        o_out[d] = summed.astype(jnp.bfloat16).reshape(2, height, latent)
        partner = {"seq": other}
        s_copies.append(go(remote(s_out.at[d, other], s_in.at[d], s_send.at[d], s_recv.at[d], partner)))
        o_copies.append(go(remote(o_out.at[d, other], o_in.at[d], o_send.at[d], o_recv.at[d], partner)))

    def merge(d):
        s_copies[d].wait_recv()
        one, two = s_out[d, core], s_in[d]
        top = jnp.maximum(one[0:1], two[0:1])
        c1, c2 = jnp.exp2(one[0:1] - top), jnp.exp2(two[0:1] - top)
        total = one[1:2] * c1 + two[1:2] * c2
        line = lax.broadcasted_iota(jnp.int32, zs_out.shape[1:], 0)
        zs_out[d] = jnp.where(line == 0, top, total)
        cols = as_columns([c1, c2], height)
        o_copies[d].wait_recv()
        merged = o_out[d, core].astype(jnp.float32) * cols[:, 0:1] + o_in[d].astype(
            jnp.float32
        ) * cols[:, 1:2]
        z_out[d] = merged.astype(jnp.bfloat16)
        if d > 0:
            there = {"branch": lax.rem(z + nb - d, nb)}
            zs_copies.append(
                go(remote(zs_out.at[d], zs_in.at[d], zs_send.at[d], zs_recv.at[d], there))
            )
            z_copies.append(go(remote(z_out.at[d], z_in.at[d], z_send.at[d], z_recv.at[d], there)))

    cache_copy.wait()
    depth = out_v.shape[1]
    out_copies = []
    for g in range(2):
        out_copies.append(
            pltpu.make_async_copy(
                out_w_ref.at[pl.ds(g * depth, depth)], out_v.at[g], local_sem.at[2 + g]
            )
        )
        out_copies[-1].start()
    forwards = [None]
    attend(0)
    for d in range(1, nb):
        q_copies[d].wait_recv()
        forward = go(
            remote(
                q_all.at[d, core], q_all.at[d, core], f_send.at[d], f_recv.at[d], {"seq": other}
            )
        )
        merge(d - 1)
        forward.wait_recv()
        attend(d)
    merge(nb - 1)

    for d in range(1, nb):
        kv_copies[d].wait_recv()
    new_keys = kv_all[...].reshape(-1, feature)
    size = height // groups
    new_scores = lax.dot_general(
        q_half(core)[...].reshape(height, feature), new_keys, (((1,), (1,)), ((), ())), preferred_element_type=jnp.float32
    )
    pad = kv_v.shape[0]
    extent = (groups, nb * pad)
    spot = lax.broadcasted_iota(jnp.int32, extent, 1)
    entry = lax.broadcasted_iota(jnp.int32, extent, 0)
    origin = z - spot // pad
    origin = jnp.where(origin < 0, origin + nb, origin)
    inner = spot % pad
    which = jnp.where(inner < groups, origin * rows + inner // 2, -2)
    above = jnp.full(extent, -1, jnp.int32)
    for r in range(rows):
        above = jnp.where(entry // 2 == r, parent_ref[z * rows + r], above)
    seen = (which == above) | ((which == z * rows + entry // 2) & (inner % 2 <= entry % 2))
    new_bias = jnp.where(seen, 0.0, LOW)
    new_v = new_scores.reshape(groups, size, -1) * scale + new_bias[:, None, :]
    new_v = new_v.reshape(height, -1)
    new_peak = jnp.max(new_v, axis=1, keepdims=True)
    new_p = jnp.exp2(new_v - new_peak)
    new_total = jnp.sum(new_p, axis=1, keepdims=True)
    new_row = pair_row(new_peak, new_total)
    new_sum = jnp.dot(
        new_p.astype(jnp.bfloat16), new_keys[:, :latent], preferred_element_type=jnp.float32
    )

    stats = [zs_out[0], new_row]
    for d in range(1, nb):
        zs_copies[d].wait_recv()
        stats.append(zs_in[d])
    top = functools.reduce(jnp.maximum, [s[0:1] for s in stats])
    shares = [jnp.exp2(s[0:1] - top) for s in stats]
    total = sum(c * s[1:2] for c, s in zip(shares, stats))
    cols = as_columns([c / total for c in shares], height)
    latent_out = z_out[0].astype(jnp.float32) * cols[:, 0:1] + new_sum * cols[:, 1:2]
    for d in range(1, nb):
        z_copies[d].wait_recv()
        latent_out = latent_out + z_in[d].astype(jnp.float32) * cols[:, d + 1 : d + 2]
    for j in range(latent // 128):
        latent_v[j] = latent_out[:, j * 128 : (j + 1) * 128]

    uv_copy.wait()
    for h in range(heads):
        part = jnp.concatenate(
            [latent_v[j, pl.ds(h, groups, stride=heads), :] for j in range(latent // 128)], axis=1
        )
        high = part.astype(jnp.bfloat16)
        rest = (part - high.astype(jnp.float32)).astype(jnp.bfloat16)
        both = jnp.dot(
            jnp.concatenate([high, rest], axis=0), uv_v[h], preferred_element_type=jnp.float32
        )
        up = both[:groups] + both[groups:]
        head_v[core, :, h * VHEAD : (h + 1) * VHEAD] = jnp.concatenate([up, up], axis=0).astype(
            jnp.bfloat16
        )
    swap = go(
        remote(head_v.at[core], head_v.at[core], h_send.at[0], h_recv.at[0], {"seq": other})
    )
    for copy in out_copies:
        copy.wait()
    result = jnp.dot(head_v[core], out_v[core], preferred_element_type=jnp.float32)
    swap.wait_recv()
    result = result + jnp.dot(head_v[other], out_v[other], preferred_element_type=jnp.float32)
    result = result[:groups]
    red_out[...] = result
    reds = []
    for e in range(1, hc):
        there = {"head": lax.rem(x + e, hc)}
        reds.append(
            go(remote(red_out, red_in.at[e - 1], r_send.at[e - 1], r_recv.at[e - 1], there))
        )
    for e in range(1, hc):
        reds[e - 1].wait_recv()
        result = result + red_in[e - 1]
    count = groups // hc
    kept = jnp.zeros((count, result.shape[1]), jnp.float32)
    for k in range(hc):
        kept = jnp.where(x == k, result[k * count : (k + 1) * count], kept)
    for k in range(count // 2):
        out_ref[k] = kept[2 * k : 2 * k + 2].astype(out_ref.dtype)
    for copy in sent:
        copy.wait_send()


def local(queries, kv_new, cache, block_list, lengths, parent, w_uv, w_out):
    rows, _, heads, feature = queries.shape
    block_count, block_len, _ = cache.shape
    latent = w_uv.shape[1]
    nb = lax.axis_size("branch")
    ns = lax.axis_size("seq")
    hc = lax.axis_size("head")
    slots = block_list.shape[1] // (nb * ns)
    scale = float(VHEAD + ROPE) ** (-0.5) * 1.4426950408889634
    half = heads // 2
    groups = rows * 2
    height = groups * half
    q = queries.reshape(groups, heads, feature)
    if half % 16 != 0:
        q = q.reshape(groups, 2, half, feature).transpose(1, 0, 2, 3)
    pad = 16
    branches = block_list.shape[0]
    depth = w_out.shape[0] // 2
    width = w_out.shape[1]
    dma = pltpu.SemaphoreType.DMA
    vmem = pl.BlockSpec(memory_space=pltpu.VMEM)
    hbm = pl.BlockSpec(memory_space=pl.ANY)
    smem = pl.BlockSpec(memory_space=pltpu.SMEM)
    bf16, f32 = jnp.bfloat16, jnp.float32
    return pl.pallas_call(
        functools.partial(kernel, scale, rows),
        out_shape=jax.ShapeDtypeStruct((rows // hc, 2, width), bf16),
        in_specs=[
            vmem,
            smem,
            smem,
            vmem,
            vmem,
            hbm,
            hbm,
            hbm,
        ],
        out_specs=vmem,
        scratch_shapes=[
            pltpu.VMEM((block_count, feature, block_len), bf16),
            pltpu.VMEM((half, latent, VHEAD), bf16),
            pltpu.VMEM((2, depth, width), bf16),
            pltpu.VMEM((nb, 2, groups, half, feature), bf16),
            pltpu.VMEM((nb, pad, feature), bf16),
            pltpu.VMEM((feature, slots * block_len), bf16),
            pltpu.VMEM((2 * height, slots * block_len), f32),
            pltpu.VMEM((2 * height, slots * block_len), bf16),
            pltpu.VMEM((2 * height, 128), f32),
            pltpu.VMEM((nb, 2, height, latent), bf16),
            pltpu.VMEM((nb, height, latent), bf16),
            pltpu.VMEM((nb, 2, 8, 128), f32),
            pltpu.VMEM((nb, 8, 128), f32),
            pltpu.VMEM((nb, height, latent), bf16),
            pltpu.VMEM((nb, height, latent), bf16),
            pltpu.VMEM((nb, 8, 128), f32),
            pltpu.VMEM((nb, 8, 128), f32),
            pltpu.VMEM((latent // 128, height, 128), f32),
            pltpu.VMEM(block_list.shape, jnp.int32),
            pltpu.SMEM(block_list.shape, jnp.int32),
            pltpu.VMEM((branches, slots * block_len), f32),
            pltpu.VMEM((pad, feature), bf16),
            pltpu.VMEM((2, 2 * groups, half * VHEAD), bf16),
            pltpu.VMEM((groups, width), f32),
            pltpu.VMEM((hc, groups, width), f32),
            dma((5,)),
        ]
        + [dma((nb,)) for _ in range(14)]
        + [dma((1,)), dma((1,)), dma((hc,)), dma((hc,))],
        compiler_params=pltpu.CompilerParams(
            collective_id=0, has_side_effects=True, vmem_limit_bytes=56 * 1024 * 1024
        ),
    )(block_list, lengths, parent, q, kv_new, cache.swapaxes(1, 2), w_uv, w_out)


def solution(mesh):
    return jax.shard_map(
        local,
        mesh=mesh,
        in_specs=(
            P(("groups", "branch"), None, "head", None),
            P(("groups", "branch"), None, None),
            P(("groups", "branch", "seq"), None, None),
            P("groups", None),
            P("groups"),
            P("groups"),
            P("head", None, None),
            P("head", "seq"),
        ),
        out_specs=P(("groups", "branch", "head"), None, "seq"),
        check_vma=False,
    )
```

```python
import functools

import jax
import jax.numpy as jnp
from jax import lax
from jax.experimental import pallas as pl
from jax.experimental.pallas import tpu as pltpu
from jax.sharding import PartitionSpec as P

ROPE = 64
VHEAD = 128
MESH = pl.DeviceIdType.MESH
LOW = -1e30


def as_row(column):
    short = 128 - column.shape[0]
    if short > 0:
        column = jnp.concatenate([column, jnp.zeros((short, 128), jnp.float32)], axis=0)
    return jnp.transpose(column)[:8]


def as_columns(rows_in, height):
    lane = lax.broadcasted_iota(jnp.int32, (128, rows_in[0].shape[1]), 0)
    stacked = jnp.zeros(lane.shape, jnp.float32)
    for j, row in enumerate(rows_in):
        stacked = jnp.where(lane == j, row[0:1], stacked)
    return jnp.transpose(stacked)[:height]


def pair_row(peak, total):
    lane = lax.broadcasted_iota(jnp.int32, (peak.shape[0], 128), 1)
    return as_row(jnp.where(lane == 0, peak, total))


def kernel(
    scale,
    rows,
    list_ref,
    lengths_ref,
    parent_ref,
    q_ref,
    kv_ref,
    cache_ref,
    uv_ref,
    out_w_ref,
    out_ref,
    cache_v,
    uv_v,
    out_v,
    q_all,
    kv_all,
    keys,
    scores,
    probs,
    column,
    o_out,
    o_in,
    s_out,
    s_in,
    z_out,
    z_in,
    zs_out,
    zs_in,
    latent_v,
    ids_v,
    ids_s,
    bias_v,
    kv_v,
    head_v,
    red_out,
    red_in,
    local_sem,
    q_send,
    q_recv,
    f_send,
    f_recv,
    kv_send,
    kv_recv,
    o_send,
    o_recv,
    s_send,
    s_recv,
    z_send,
    z_recv,
    zs_send,
    zs_recv,
    h_send,
    h_recv,
    r_send,
    r_recv,
):
    nb, hc = lax.axis_size("branch"), lax.axis_size("head")
    z, x, core = lax.axis_index("branch"), lax.axis_index("head"), lax.axis_index("seq")
    other = 1 - core
    block_count, feature, block_len = cache_v.shape
    branches, list_len = list_ref.shape
    slots = list_len // (nb * 2)
    latent = uv_v.shape[1]
    heads = uv_v.shape[0]
    groups = rows * 2
    height = groups * heads

    def q_half(g):
        if len(q_ref.shape) == 4:
            return q_ref.at[g]
        return q_ref.at[:, pl.ds(pl.multiple_of(g * heads, heads), heads), :]

    cache_copy = pltpu.make_async_copy(cache_ref, cache_v, local_sem.at[0])
    cache_copy.start()
    uv_copy = pltpu.make_async_copy(uv_ref.at[pl.ds(core * heads, heads)], uv_v, local_sem.at[1])
    uv_copy.start()
    barrier = pltpu.get_barrier_semaphore()
    for d in range(1, nb):
        pl.semaphore_signal(
            barrier, inc=1, device_id={"branch": lax.rem(z + d, nb)}, device_id_type=MESH
        )
    for e in range(1, hc):
        pl.semaphore_signal(
            barrier, inc=1, device_id={"head": lax.rem(x + e, hc)}, device_id_type=MESH
        )
    pl.semaphore_signal(barrier, inc=1, device_id={"seq": other}, device_id_type=MESH)

    drafts = [kv_ref[r].astype(jnp.float32) for r in range(rows)]
    drafts.append(jnp.zeros((kv_v.shape[0] - groups, feature), jnp.float32))
    kv_v[...] = jnp.concatenate(drafts, axis=0).astype(jnp.bfloat16)
    pl.semaphore_wait(barrier, nb - 1 + hc - 1 + 1)

    def remote(src, dst, send, recv, target):
        return pltpu.make_async_remote_copy(
            src_ref=src,
            dst_ref=dst,
            send_sem=send,
            recv_sem=recv,
            device_id=target,
            device_id_type=MESH,
        )

    sent = []

    def go(copy):
        copy.start()
        sent.append(copy)
        return copy

    kv_copies = [None]

    def pass_on(d, act):
        block = q_half(core) if d is None else q_all.at[d, core]
        for way in (1, -1):
            if d is None:
                going = (z + 1 < nb) if way == 1 else (z > 0)
                slot = 1 if way == 1 else nb - 1
                sem = q_send.at[0] if way == 1 else q_send.at[nb]
            else:
                going = ((z >= d) & (z + 1 < nb)) if way == 1 else ((z < d) & (z > 0))
                slot = jnp.clip(d + way, 1, nb - 1)
                sem = q_send.at[d]
            there = {"branch": jnp.clip(z + way, 0, nb - 1)}

            @pl.when(going)
            def _():
                act(remote(block, q_all.at[slot, core], sem, q_recv.at[slot], there))

    fewer = jnp.minimum(z, nb - 1 - z)
    left_more = z > nb - 1 - z

    def nth(j):
        pair = (j + 1) // 2
        paired = pair if j % 2 == 1 else nb - pair
        tail = jnp.where(left_more, j - fewer, nb - (j - fewer))
        return jnp.where(j <= 2 * fewer, paired, tail)

    order = [0] + [nth(j) for j in range(1, nb)]
    pass_on(None, lambda copy: copy.start())
    for d in range(1, nb):
        there = {"branch": lax.rem(z + d, nb)}
        kv_copies.append(go(remote(kv_v, kv_all.at[d], kv_send.at[d], kv_recv.at[d], there)))
    kv_all[0] = kv_v[...]

    mine = list_ref[...] - (z * 2 + core) * block_count
    lead = jnp.concatenate(
        [
            jnp.broadcast_to(mine[i * rows : i * rows + 1], (rows, list_len))
            for i in range(nb)
        ],
        axis=0,
    )
    held = (lead >= 0) & (lead < block_count)
    spots = lax.broadcasted_iota(jnp.int32, (branches, list_len), 1)
    line = lax.broadcasted_iota(jnp.int32, (branches, list_len), 0)
    counted = held.astype(jnp.int32)
    rank = counted
    step = 1
    while step < list_len:
        rank = rank + jnp.where(spots >= step, pltpu.roll(rank, step, 1), 0)
        step *= 2
    rank = jnp.where(held, rank - 1, -1)
    reach = jnp.zeros((branches, list_len), jnp.int32)
    for b in range(branches):
        reach = jnp.where(line == b, lengths_ref[b], reach)
    table = jnp.zeros((branches, list_len), jnp.int32)
    picks = []
    for s in range(slots):
        pick = jnp.sum(jnp.where(rank == s, lead, 0), axis=1, keepdims=True)
        picks.append(pick)
        table = jnp.where(spots == s, pick, table)
    ids_v[...] = table
    ids_copy = pltpu.make_async_copy(ids_v, ids_s, local_sem.at[4])
    ids_copy.start()
    for s in range(slots):
        place = jnp.sum(jnp.where(mine == picks[s], spots, 0), axis=1, keepdims=True)
        seen = spots + place * block_len < reach
        bias_v[:, s * block_len : (s + 1) * block_len] = jnp.where(seen, 0.0, LOW)
    ids_copy.wait()

    o_copies, s_copies, z_copies, zs_copies = [], [], [None], [None]

    def attend(j):
        d = order[j]
        source = lax.rem(z + nb - d, nb)
        for s in range(slots):
            keys[:, s * block_len : (s + 1) * block_len] = cache_v[ids_s[source * rows, s]]
        if j == 0:
            q = jnp.concatenate(
                [q_half(g)[...].reshape(height, feature) for g in range(2)], axis=0
            )
        else:
            q = q_all[d].reshape(2 * height, feature)
        scores[...] = jnp.dot(q, keys[...], preferred_element_type=jnp.float32)
        size = height // rows
        for g in range(2):
            for r in range(rows):
                at = g * height + r * size
                v = scores[at : at + size, :] * scale + bias_v[pl.ds(source * rows + r, 1), :]
                peak = jnp.max(v, axis=1, keepdims=True)
                p = jnp.exp2(v - peak)
                total = jnp.sum(p, axis=1, keepdims=True)
                probs[at : at + size, :] = p.astype(jnp.bfloat16)
                lane = lax.broadcasted_iota(jnp.int32, (size, 128), 1)
                column[at : at + size, :] = jnp.where(lane == 0, peak, total)
        for g in range(2):
            s_out[d, g] = as_row(column[g * height : (g + 1) * height, :])
        summed = lax.dot_general(
            probs[...],
            keys[:latent, :],
            (((1,), (1,)), ((), ())),
            preferred_element_type=jnp.float32,
        )
        o_out[d] = summed.astype(jnp.bfloat16).reshape(2, height, latent)
        partner = {"seq": other}
        s_copies.append(go(remote(s_out.at[d, other], s_in.at[d], s_send.at[d], s_recv.at[d], partner)))
        o_copies.append(go(remote(o_out.at[d, other], o_in.at[d], o_send.at[d], o_recv.at[d], partner)))

    def merge(j):
        d = order[j]
        s_copies[j].wait_recv()
        one, two = s_out[d, core], s_in[d]
        top = jnp.maximum(one[0:1], two[0:1])
        c1, c2 = jnp.exp2(one[0:1] - top), jnp.exp2(two[0:1] - top)
        total = one[1:2] * c1 + two[1:2] * c2
        line = lax.broadcasted_iota(jnp.int32, zs_out.shape[1:], 0)
        zs_out[d] = jnp.where(line == 0, top, total)
        cols = as_columns([c1, c2], height)
        o_copies[j].wait_recv()
        merged = o_out[d, core].astype(jnp.float32) * cols[:, 0:1] + o_in[d].astype(
            jnp.float32
        ) * cols[:, 1:2]
        z_out[d] = merged.astype(jnp.bfloat16)
        if j > 0:
            there = {"branch": lax.rem(z + nb - d, nb)}
            zs_copies.append(
                go(remote(zs_out.at[d], zs_in.at[d], zs_send.at[d], zs_recv.at[d], there))
            )
            z_copies.append(go(remote(z_out.at[d], z_in.at[d], z_send.at[d], z_recv.at[d], there)))

    cache_copy.wait()
    depth = out_v.shape[1]
    out_copies = []
    for g in range(2):
        out_copies.append(
            pltpu.make_async_copy(
                out_w_ref.at[pl.ds(g * depth, depth)], out_v.at[g], local_sem.at[2 + g]
            )
        )
        out_copies[-1].start()
    forwards = [None]

    def receive(j):
        d = order[j]
        landed = q_all.at[d, core]
        remote(landed, landed, q_send.at[d], q_recv.at[d], {"seq": other}).wait_recv()
        pass_on(d, lambda copy: copy.start())
        forwards.append(go(remote(landed, landed, f_send.at[d], f_recv.at[d], {"seq": other})))

    attend(0)
    receive(1)
    for j in range(1, nb):
        if j + 1 < nb:
            receive(j + 1)
        merge(j - 1)
        forwards[j].wait_recv()
        attend(j)
    merge(nb - 1)

    for d in range(1, nb):
        kv_copies[d].wait_recv()
    new_keys = kv_all[...].reshape(-1, feature)
    size = height // groups
    new_scores = lax.dot_general(
        q_half(core)[...].reshape(height, feature), new_keys, (((1,), (1,)), ((), ())), preferred_element_type=jnp.float32
    )
    pad = kv_v.shape[0]
    extent = (groups, nb * pad)
    spot = lax.broadcasted_iota(jnp.int32, extent, 1)
    entry = lax.broadcasted_iota(jnp.int32, extent, 0)
    origin = z - spot // pad
    origin = jnp.where(origin < 0, origin + nb, origin)
    inner = spot % pad
    which = jnp.where(inner < groups, origin * rows + inner // 2, -2)
    above = jnp.full(extent, -1, jnp.int32)
    for r in range(rows):
        above = jnp.where(entry // 2 == r, parent_ref[z * rows + r], above)
    seen = (which == above) | ((which == z * rows + entry // 2) & (inner % 2 <= entry % 2))
    new_bias = jnp.where(seen, 0.0, LOW)
    new_v = new_scores.reshape(groups, size, -1) * scale + new_bias[:, None, :]
    new_v = new_v.reshape(height, -1)
    new_peak = jnp.max(new_v, axis=1, keepdims=True)
    new_p = jnp.exp2(new_v - new_peak)
    new_total = jnp.sum(new_p, axis=1, keepdims=True)
    new_row = pair_row(new_peak, new_total)
    new_sum = jnp.dot(
        new_p.astype(jnp.bfloat16), new_keys[:, :latent], preferred_element_type=jnp.float32
    )

    stats = [zs_out[0], new_row]
    for d in range(1, nb):
        remote(zs_out.at[d], zs_in.at[d], zs_send.at[d], zs_recv.at[d], {"seq": other}).wait_recv()
        stats.append(zs_in[d])
    top = functools.reduce(jnp.maximum, [s[0:1] for s in stats])
    shares = [jnp.exp2(s[0:1] - top) for s in stats]
    total = sum(c * s[1:2] for c, s in zip(shares, stats))
    cols = as_columns([c / total for c in shares], height)
    latent_out = z_out[0].astype(jnp.float32) * cols[:, 0:1] + new_sum * cols[:, 1:2]
    for d in range(1, nb):
        remote(z_out.at[d], z_in.at[d], z_send.at[d], z_recv.at[d], {"seq": other}).wait_recv()
        latent_out = latent_out + z_in[d].astype(jnp.float32) * cols[:, d + 1 : d + 2]
    for j in range(latent // 128):
        latent_v[j] = latent_out[:, j * 128 : (j + 1) * 128]

    uv_copy.wait()
    for h in range(heads):
        part = jnp.concatenate(
            [latent_v[j, pl.ds(h, groups, stride=heads), :] for j in range(latent // 128)], axis=1
        )
        high = part.astype(jnp.bfloat16)
        rest = (part - high.astype(jnp.float32)).astype(jnp.bfloat16)
        both = jnp.dot(
            jnp.concatenate([high, rest], axis=0), uv_v[h], preferred_element_type=jnp.float32
        )
        up = both[:groups] + both[groups:]
        head_v[core, :, h * VHEAD : (h + 1) * VHEAD] = jnp.concatenate([up, up], axis=0).astype(
            jnp.bfloat16
        )
    swap = go(
        remote(head_v.at[core], head_v.at[core], h_send.at[0], h_recv.at[0], {"seq": other})
    )
    for copy in out_copies:
        copy.wait()
    result = jnp.dot(head_v[core], out_v[core], preferred_element_type=jnp.float32)
    swap.wait_recv()
    result = result + jnp.dot(head_v[other], out_v[other], preferred_element_type=jnp.float32)
    result = result[:groups]
    red_out[...] = result
    reds = []
    for e in range(1, hc):
        there = {"head": lax.rem(x + e, hc)}
        reds.append(
            go(remote(red_out, red_in.at[e - 1], r_send.at[e - 1], r_recv.at[e - 1], there))
        )
    for e in range(1, hc):
        reds[e - 1].wait_recv()
        result = result + red_in[e - 1]
    count = groups // hc
    kept = jnp.zeros((count, result.shape[1]), jnp.float32)
    for k in range(hc):
        kept = jnp.where(x == k, result[k * count : (k + 1) * count], kept)
    for k in range(count // 2):
        out_ref[k] = kept[2 * k : 2 * k + 2].astype(out_ref.dtype)
    for copy in sent:
        copy.wait_send()
    pass_on(None, lambda copy: copy.wait_send())
    for j in range(1, nb):
        pass_on(order[j], lambda copy: copy.wait_send())


def local(queries, kv_new, cache, block_list, lengths, parent, w_uv, w_out):
    rows, _, heads, feature = queries.shape
    block_count, block_len, _ = cache.shape
    latent = w_uv.shape[1]
    nb = lax.axis_size("branch")
    ns = lax.axis_size("seq")
    hc = lax.axis_size("head")
    slots = block_list.shape[1] // (nb * ns)
    scale = float(VHEAD + ROPE) ** (-0.5) * 1.4426950408889634
    half = heads // 2
    groups = rows * 2
    height = groups * half
    q = queries.reshape(groups, heads, feature)
    if half % 16 != 0:
        q = q.reshape(groups, 2, half, feature).transpose(1, 0, 2, 3)
    pad = 16
    branches = block_list.shape[0]
    depth = w_out.shape[0] // 2
    width = w_out.shape[1]
    dma = pltpu.SemaphoreType.DMA
    vmem = pl.BlockSpec(memory_space=pltpu.VMEM)
    hbm = pl.BlockSpec(memory_space=pl.ANY)
    smem = pl.BlockSpec(memory_space=pltpu.SMEM)
    bf16, f32 = jnp.bfloat16, jnp.float32
    return pl.pallas_call(
        functools.partial(kernel, scale, rows),
        out_shape=jax.ShapeDtypeStruct((rows // hc, 2, width), bf16),
        in_specs=[
            vmem,
            smem,
            smem,
            vmem,
            vmem,
            hbm,
            hbm,
            hbm,
        ],
        out_specs=vmem,
        scratch_shapes=[
            pltpu.VMEM((block_count, feature, block_len), bf16),
            pltpu.VMEM((half, latent, VHEAD), bf16),
            pltpu.VMEM((2, depth, width), bf16),
            pltpu.VMEM((nb, 2, groups, half, feature), bf16),
            pltpu.VMEM((nb, pad, feature), bf16),
            pltpu.VMEM((feature, slots * block_len), bf16),
            pltpu.VMEM((2 * height, slots * block_len), f32),
            pltpu.VMEM((2 * height, slots * block_len), bf16),
            pltpu.VMEM((2 * height, 128), f32),
            pltpu.VMEM((nb, 2, height, latent), bf16),
            pltpu.VMEM((nb, height, latent), bf16),
            pltpu.VMEM((nb, 2, 8, 128), f32),
            pltpu.VMEM((nb, 8, 128), f32),
            pltpu.VMEM((nb, height, latent), bf16),
            pltpu.VMEM((nb, height, latent), bf16),
            pltpu.VMEM((nb, 8, 128), f32),
            pltpu.VMEM((nb, 8, 128), f32),
            pltpu.VMEM((latent // 128, height, 128), f32),
            pltpu.VMEM(block_list.shape, jnp.int32),
            pltpu.SMEM(block_list.shape, jnp.int32),
            pltpu.VMEM((branches, slots * block_len), f32),
            pltpu.VMEM((pad, feature), bf16),
            pltpu.VMEM((2, 2 * groups, half * VHEAD), bf16),
            pltpu.VMEM((groups, width), f32),
            pltpu.VMEM((hc, groups, width), f32),
            dma((5,)),
        ]
        + [dma((nb + 1,)) for _ in range(14)]
        + [dma((1,)), dma((1,)), dma((hc,)), dma((hc,))],
        compiler_params=pltpu.CompilerParams(
            collective_id=0, has_side_effects=True, vmem_limit_bytes=56 * 1024 * 1024
        ),
    )(block_list, lengths, parent, q, kv_new, cache.swapaxes(1, 2), w_uv, w_out)


def solution(mesh):
    return jax.shard_map(
        local,
        mesh=mesh,
        in_specs=(
            P(("groups", "branch"), None, "head", None),
            P(("groups", "branch"), None, None),
            P(("groups", "branch", "seq"), None, None),
            P("groups", None),
            P("groups"),
            P("groups"),
            P("head", None, None),
            P("head", "seq"),
        ),
        out_specs=P(("groups", "branch", "head"), None, "seq"),
        check_vma=False,
    )
```
